32 devices in a mesh: firm: 8 (over z, y), tm: 4 (over x, core).
Axes of the slice: x: 2, y: 2, z: 4, core: 2. Of those that a mesh axis runs over, the one named last changes fastest.
Arguments:
- features: bfloat16 [4096, 8, 128], P('firm', 'tm'), may hold values from -6 to 6
- cotangent: bfloat16 [4096, 8, 128], P('firm', 'tm'), may hold values from -6 to 6
- tiles: bfloat16 [32, 32, 128, 128], P('firm'), may hold values from -0.1875 to 0.1875
- mask: int32 [32, 32], P('firm'), may hold values 0 or 1
- w_prev: bfloat16 [2, 128, 256], replicated, may hold values from -0.375 to 0.375
- w_cur: bfloat16 [2, 128, 256], replicated, may hold values from -0.375 to 0.375
- w_self: bfloat16 [2, 128, 128], replicated, may hold values from -0.5 to 0.5
- w_nbr: bfloat16 [2, 128, 128], replicated, may hold values from -0.5 to 0.5
- dilations: int32 [2], replicated, may hold values from 1 to 2, as said below
Outputs:
- grad_features: float32 [4096, 8, 128], P('firm', 'tm')
- grad_prev: float32 [2, 128, 256], replicated
- grad_cur: float32 [2, 128, 256], replicated
- grad_self: float32 [2, 128, 128], replicated
- grad_nbr: float32 [2, 128, 128], replicated
The draws below stay inside these ranges and needn't reach their ends.
Inputs may be any that keep to these rules, and one draw needn't show every extreme that they name: `dilations`: each layer's dilation lies between 1 and 2; some layer has dilation 1 and some layer has dilation 2.
All inputs are finite; a program needn't handle non-finite values. No bound on the sum of `mask` on one device may be relied on, other than what follows from the above.
Results may differ from the reference program's by a relative error of at most 0.007.
Values may be sent and summed in bfloat16 or wider, within the bound.
A program may use at most 128 MiB of HBM per device.

```python
import jax
import jax.numpy as jnp
from jax import lax

DD = 2
BS = 128
C = 128
L = 2
NB = 32
NF = 4096
DAYS = 8


def draw_dilations(key, part):
    base = jax.random.randint(jax.random.fold_in(key, 11), (L,), 1, DD + 1)
    chosen = jax.random.randint(jax.random.fold_in(key, 12), (), 0, L)
    second = (chosen + 1) % L
    layer_ids = jnp.arange(L)
    base = jnp.where(layer_ids == second, 1, base)
    return jnp.where(layer_ids == chosen, DD, base).astype(jnp.int32)


def set_ends(result, stream_key, least, top_value):
    index_at = [jax.random.randint(jax.random.fold_in(stream_key, axis), (), 0, length) for axis, length in enumerate(result.shape)]
    main_axis = result.shape.index(max(result.shape))
    beside = index_at[:main_axis] + [(index_at[main_axis] + 1) % result.shape[main_axis]] + index_at[main_axis + 1:]
    return result.at[tuple(index_at)].set(least).at[tuple(beside)].set(top_value)


def steps_of(own_key, extent, split, smallest, largest):
    def one(position, shards_of):
        draws = jax.random.uniform(jax.random.fold_in(jax.random.fold_in(own_key, 6), position), (shards_of,), jnp.float32, smallest / len(split), largest / len(split))
        return jnp.repeat(jnp.exp(draws), extent[position] // shards_of).reshape((-1,) + (1,) * (len(extent) - position - 1))

    gain = one(*split[0])
    for cut in split[1:]:
        gain = gain * one(*cut)
    return gain


def normal_values(rng, dims, width, limit, pieces=(), kind=jnp.bfloat16):
    loudness = steps_of(rng, dims, pieces, -0.22, 0.18) if pieces else 1.0
    array = jax.random.normal(rng, dims, jnp.float32) * width * loudness
    return jnp.minimum(jnp.maximum(array, -limit), limit).astype(kind)


def setup_inputs(seed: int = 0) -> dict:
    streams_of = jax.random.split(jax.random.key(seed), 10)
    features = normal_values(streams_of[0], (NF, DAYS, C), 1.0, 6.0, ((0, 8), (1, 4)))
    cotangent = normal_values(streams_of[1], (NF, DAYS, C), 1.0, 6.0, ((0, 8), (1, 4)))
    tiles = normal_values(streams_of[2], (NB, NB, BS, BS), (NB * BS // 4) ** -0.5, 0.1875, ((0, 8),))
    mask = set_ends((jax.random.randint(streams_of[3], (NB, NB), 0, 4) < 1).astype(jnp.int32), jax.random.fold_in(streams_of[3], 1), 0, 1)
    w_prev = normal_values(streams_of[4], (L, C, 2 * C), (2 * C) ** -0.5, 0.375)
    w_cur = normal_values(streams_of[5], (L, C, 2 * C), (2 * C) ** -0.5, 0.375)
    w_self = normal_values(streams_of[6], (L, C, C), C ** -0.5, 0.5)
    w_nbr = normal_values(streams_of[7], (L, C, C), C ** -0.5, 0.5)
    dilations = draw_dilations(jax.random.fold_in(streams_of[9], 71), 0)
    return dict(features=features, cotangent=cotangent, tiles=tiles, mask=mask, w_prev=w_prev, w_cur=w_cur, w_self=w_self, w_nbr=w_nbr, dilations=dilations)


def earlier_offset(x, d):
    pad = jnp.zeros((x.shape[0], DD, x.shape[2]), x.dtype)
    paired_terms = jnp.concatenate([pad, x], axis=1)
    return lax.dynamic_slice_in_dim(paired_terms, (DD - d).astype(jnp.int32), DAYS, 1)

def later_offset(x, d):
    pad = jnp.zeros((x.shape[0], DD, x.shape[2]), x.dtype)
    paired_terms = jnp.concatenate([x, pad], axis=1)
    return lax.dynamic_slice_in_dim(paired_terms, d.astype(jnp.int32), DAYS, 1)

def reference(features, cotangent, tiles, mask, w_prev, w_cur, w_self, w_nbr, dilations):
    adjacency = (tiles * mask.astype(tiles.dtype)[:, :, None, None]).transpose(0, 2, 1, 3).reshape(NF, NF)
    saved = []
    hidden_state = features
    for layer_index in range(L):
        dilation_factor = dilations[layer_index]
        previous_state = earlier_offset(hidden_state, dilation_factor)
        pre = jnp.dot(previous_state.reshape(-1, C), w_prev[layer_index], preferred_element_type=jnp.float32)
        pre = pre + jnp.dot(hidden_state.reshape(-1, C), w_cur[layer_index], preferred_element_type=jnp.float32)
        filt = pre[:, :C]
        gate = pre[:, C:]
        gated = (jnp.tanh(filt) * jax.nn.sigmoid(gate)).astype(jnp.bfloat16)
        diffused = jnp.dot(adjacency, gated.reshape(NF, DAYS * C), preferred_element_type=jnp.float32).astype(jnp.bfloat16)
        mixed = jnp.dot(gated, w_self[layer_index], preferred_element_type=jnp.float32)
        mixed = mixed + jnp.dot(diffused.reshape(-1, C), w_nbr[layer_index], preferred_element_type=jnp.float32)
        saved.append((hidden_state, previous_state, filt, gate, gated, diffused))
        hidden_state = (hidden_state.astype(jnp.float32) + mixed.reshape(NF, DAYS, C)).astype(jnp.bfloat16)
    gradient_value = cotangent.astype(jnp.float32)
    outs_prev, outs_cur, outs_self, outs_nbr = ([], [], [], [])
    for layer_index in reversed(range(L)):
        hidden_state, previous_state, filt, gate, gated, diffused = saved[layer_index]
        dilation_factor = dilations[layer_index]
        gzb = gradient_value.astype(jnp.bfloat16).reshape(-1, C)
        outs_self.append(jnp.dot(gated.T, gzb, preferred_element_type=jnp.float32))
        outs_nbr.append(jnp.dot(diffused.reshape(-1, C).T, gzb, preferred_element_type=jnp.float32))
        gdiff = jnp.dot(gzb, w_nbr[layer_index].T, preferred_element_type=jnp.float32).astype(jnp.bfloat16)
        ggated = jnp.dot(gzb, w_self[layer_index].T, preferred_element_type=jnp.float32)
        spread = jnp.dot(adjacency.T, gdiff.reshape(NF, DAYS * C), preferred_element_type=jnp.float32)
        ggated = ggated + spread.reshape(-1, C)
        th = jnp.tanh(filt)
        sg = jax.nn.sigmoid(gate)
        gpre = jnp.concatenate([ggated * sg * (1.0 - th * th), ggated * th * sg * (1.0 - sg)], axis=1).astype(jnp.bfloat16)
        outs_cur.append(jnp.dot(hidden_state.reshape(-1, C).T, gpre, preferred_element_type=jnp.float32))
        outs_prev.append(jnp.dot(previous_state.reshape(-1, C).T, gpre, preferred_element_type=jnp.float32))
        reverse_flow = jnp.dot(gpre, w_prev[layer_index].T, preferred_element_type=jnp.float32).reshape(NF, DAYS, C)
        direct_path = jnp.dot(gpre, w_cur[layer_index].T, preferred_element_type=jnp.float32).reshape(NF, DAYS, C)
        gradient_value = gradient_value + direct_path + later_offset(reverse_flow, dilation_factor)
    factor = 1.0 / jnp.sqrt(jnp.float32(NF * DAYS))
    return (gradient_value, jnp.stack(outs_prev[::-1]) * factor, jnp.stack(outs_cur[::-1]) * factor, jnp.stack(outs_self[::-1]) * factor, jnp.stack(outs_nbr[::-1]) * factor)
```

```python
import functools

import jax
import jax.numpy as jnp
from jax import lax
from jax.experimental import pallas as pl
from jax.experimental.pallas import tpu as pltpu
from jax.sharding import PartitionSpec as P

L = 2
BF = jnp.bfloat16
F32 = jnp.float32


def dot(a, b, ca=1, cb=0):
    return lax.dot_general(a, b, (((ca,), (cb,)), ((), ())), preferred_element_type=F32)


def body(n, m, short_fast, factor, x_ref, cot_ref, tiles_ref, mask_ref, wp_ref, wc_ref, ws_ref,
         wn_ref, dil_ref, gx_ref, op_ref, oc_ref, os_ref, on_ref, adj, x1, gat, th, sg, zt, acc, gx,
         prv, gpre, halo, back, nxt, ag_r, ag_l, rs_out, rs_in, gp, r1, s2, fin, send, recv):
    rows, wide = x_ref.shape
    c = wide // 2
    half = n // 2
    f = lax.axis_index("firm")
    t = lax.axis_index("tm")
    if short_fast:
        fy, fz = f % 2, f // 2
    else:
        fy, fz = f // half, f % half
    pos = fz + fy * (n - 1 - 2 * fz)

    def firm_at(p):
        p = (p + 2 * n) % n
        y = p // half
        z = p + y * (n - 1 - 2 * p)
        return 2 * z + y if short_fast else y * half + z

    right = firm_at(pos + 1)
    left = firm_at(pos - 1)
    later = (t + 1) % m
    sooner = (t + m - 1) % m
    started = []

    def copy(src, dst, firm=None, tm=None):
        i = len(started)
        cp = pltpu.make_async_remote_copy(
            src_ref=src, dst_ref=dst, send_sem=send.at[i], recv_sem=recv.at[i],
            device_id=(f if firm is None else firm, t if tm is None else tm),
            device_id_type=pl.DeviceIdType.MESH)
        cp.start()
        started.append(cp)
        return cp

    barrier = pltpu.get_barrier_semaphore()
    for o in range(1, n):
        pl.semaphore_signal(barrier, inc=1, device_id=((f + o) % n, t),
                            device_id_type=pl.DeviceIdType.MESH)
    for o in range(1, m):
        pl.semaphore_signal(barrier, inc=1, device_id=(f, (t + o) % m),
                            device_id_type=pl.DeviceIdType.MESH)
    pl.semaphore_wait(barrier, n + m - 2)

    def day(k):
        return slice(k * c, (k + 1) * c)

    def block(q):
        return pl.ds(pl.multiple_of(firm_at(q) * rows, rows), rows)

    halo_cp = copy(x_ref, halo.at[0], tm=later)

    def build(j, _):
        cols = pl.ds(pl.multiple_of(j * c, c), c)
        for i in range(tiles_ref.shape[0]):
            keep = mask_ref[i, j].astype(F32)
            adj[i * c:(i + 1) * c, cols] = (tiles_ref[i, j].astype(F32) * keep).astype(BF)
        return 0

    lax.fori_loop(0, tiles_ref.shape[1], build, 0)

    class Scatter:
        def __init__(self, w):
            self.w, self.cps = w, []

        def part(self, q):
            return dot(zt[self.w], adj[:, block(q)])

        def begin(self):
            p = self.part(pos + half).astype(BF)
            out = rs_out.at[self.w, 0, 0]
            out[...] = p
            top, low = pl.ds(0, c), pl.ds(c, c)
            self.cps.append((
                copy(out.at[top], rs_in.at[self.w, 0, 0, top], firm=right),
                copy(out.at[low], rs_in.at[self.w, 1, 0, low], firm=left)))

        def step(self, k):
            new = []
            for dr in range(2):
                p = self.part(pos + (half - k) * (1 - 2 * dr))
                self.cps[k - 1][dr].wait_recv()
                out = rs_out.at[self.w, dr, k]
                if k == 1:
                    got = slice(dr * c, (dr + 1) * c)
                    own = slice((1 - dr) * c, (2 - dr) * c)
                    out[got, :] = (p[got] + rs_in[self.w, dr, 0, got].astype(F32)).astype(BF)
                    out[own, :] = p[own].astype(BF)
                else:
                    out[...] = (p + rs_in[self.w, dr, k - 1].astype(F32)).astype(BF)
                new.append(copy(out, rs_in.at[self.w, dr, k], firm=(right, left)[dr]))
            self.cps.append(new)

        def end(self):
            p = self.part(pos)
            for dr in range(2):
                self.cps[half - 1][dr].wait_recv()
                p = p + rs_in[self.w, dr, half - 1].astype(F32)
            return p.T.astype(BF)

    def forward(l, x):
        d1 = dil_ref[l] == 1
        h = halo[l].astype(F32)
        h = h * jnp.where(t > 0, 1.0, 0.0)
        one = jnp.where(d1, 1.0, 0.0)
        h0, h1 = h[:, day(0)], h[:, day(1)]
        prv[l, :, day(0)] = (h1 * one + h0 * (1.0 - one)).astype(BF)
        prv[l, :, day(1)] = (x[:, day(0)].astype(F32) * one + h1 * (1.0 - one)).astype(BF)
        for k in range(2):
            pre = dot(prv[l, :, day(k)], wp_ref[l]) + dot(x[:, day(k)], wc_ref[l])
            a = jnp.tanh(pre[:, :c])
            b = 0.5 * jnp.tanh(0.5 * pre[:, c:]) + 0.5
            th[l, :, day(k)] = a
            sg[l, :, day(k)] = b
            gat[l, :, day(k)] = (a * b).astype(BF)

    def pre_grad(l, zb, u):
        for k in range(2):
            gg = dot(zb[:, day(k)], ws_ref[l], 1, 1) + dot(u[:, day(k)], wn_ref[l], 1, 1)
            a, b = th[l, :, day(k)], sg[l, :, day(k)]
            gpre[k, :, :c] = (gg * b * (1.0 - a * a)).astype(BF)
            gpre[k, :, c:] = (gg * a * b * (1.0 - b)).astype(BF)
            back[l, :, day(k)] = dot(gpre[k], wp_ref[l], 1, 1).astype(BF)

    def direct(l, k):
        return dot(gpre[k], wc_ref[l], 1, 1)

    def shifted(l):
        one = jnp.where(dil_ref[l] == 1, 1.0, 0.0)
        nb = nxt[l].astype(F32) * jnp.where(t < m - 1, 1.0, 0.0)
        n0, n1 = nb[:, day(0)], nb[:, day(1)]
        b1 = back[l, :, day(1)].astype(F32)
        return (b1 * one + n0 * (1.0 - one), n0 * one + n1 * (1.0 - one))

    def weight_grads(l, x, zb, u):
        def total(a, b):
            return dot(a[:, day(0)], b[0], 0, 0) + dot(a[:, day(1)], b[1], 0, 0)

        pieces = []
        g2 = (gpre[0], gpre[1])
        for w in (total(prv[l], g2), total(x, g2)):
            pieces += [w[:, :c], w[:, c:]]
        z2 = (zb[:, day(0)], zb[:, day(1)])
        u2 = (u[:, day(0)], u[:, day(1)])
        pieces += [total(gat[l], z2), total(gat[l], u2)]
        gp[l] = jnp.concatenate(pieces, axis=0).astype(BF).reshape(gp.shape[1:])

    class Total:
        def __init__(self, l):
            self.l = l

        def first(self):
            self.a = [copy(gp.at[self.l, (f + o) % n], r1.at[self.l, o - 1], firm=(f + o) % n)
                      for o in range(1, n)]

        def second(self):
            l = self.l
            s = gp[l, f].astype(F32)
            for o in range(1, n):
                self.a[o - 1].wait_recv()
                s = s + r1[l, o - 1].astype(F32)
            s2[l, t] = s.astype(BF)
            self.b = [copy(s2.at[l, t], s2.at[l, t], tm=(t + o) % m) for o in range(1, m)]

        def third(self):
            l = self.l
            for cp in self.b:
                cp.wait_recv()
            s = s2[l, 0].astype(F32)
            for j in range(1, m):
                s = s + s2[l, j].astype(F32)
            fin[l, f] = s.astype(BF)
            self.d = [copy(fin.at[l, f], fin.at[l, f], firm=(f + o) % n) for o in range(1, n)]

        def last(self):
            l = self.l
            for cp in self.d:
                cp.wait_recv()
            g = fin[l].reshape(6 * c, c).astype(F32) * factor
            op_ref[l, :, :c] = g[:c]
            op_ref[l, :, c:] = g[c:2 * c]
            oc_ref[l, :, :c] = g[2 * c:3 * c]
            oc_ref[l, :, c:] = g[3 * c:4 * c]
            os_ref[l] = g[4 * c:5 * c]
            on_ref[l] = g[5 * c:]

    zt[1] = cot_ref[...].astype(F32).T.astype(BF)
    rs1 = Scatter(1)
    rs1.begin()
    halo_cp.wait_recv()
    x0 = x_ref[...]
    forward(0, x0)

    cps = [(copy(gat.at[0], ag_r.at[0], firm=right), copy(gat.at[0], ag_l.at[0], firm=left))]
    acc[...] = dot(adj[:, block(pos)], gat[0])
    for s in range(1, half + 1):
        new = []
        for dr, (buf, to) in enumerate(((ag_r, right), (ag_l, left))):
            cps[s - 1][dr].wait_recv()
            if s < half - 1:
                new.append(copy(buf.at[s - 1], buf.at[s], firm=to))
            elif s == half - 1:
                part = pl.ds(dr * (rows // 2), rows // 2)
                new.append(copy(buf.at[s - 1, part], buf.at[s, part], firm=to))
        cps.append(new)
        if s < half:
            acc[...] += (dot(adj[:, block(pos - s)], ag_r[s - 1])
                         + dot(adj[:, block(pos + s)], ag_l[s - 1]))
            if s < half - 1:
                rs1.step(s)
        else:
            h = rows // 2
            far = firm_at(pos + half) * rows
            acc[...] += (dot(adj[:, pl.ds(pl.multiple_of(far, h), h)], ag_r[s - 1, :h])
                         + dot(adj[:, pl.ds(pl.multiple_of(far + h, h), h)], ag_l[s - 1, h:]))
    for k in range(2):
        mixed = (dot(gat[0, :, day(k)], ws_ref[0])
                 + dot(acc[:, day(k)].astype(BF), wn_ref[0]))
        x1[:, day(k)] = (x_ref[:, day(k)].astype(F32) + mixed).astype(BF)
    halo_cp = copy(x1, halo.at[1], tm=later)
    rs1.step(half - 1)
    halo_cp.wait_recv()
    forward(1, x1[...])

    cot = cot_ref[...]
    u = rs1.end()
    pre_grad(1, cot, u)
    back_cp = copy(back.at[1], nxt.at[1], tm=sooner)
    weight_grads(1, x1[...], cot, u)
    for k in range(2):
        gx[:, day(k)] = cot[:, day(k)].astype(F32) + direct(1, k)
    back_cp.wait_recv()
    sh = shifted(1)
    for k in range(2):
        gx[:, day(k)] = gx[:, day(k)] + sh[k]
    zb = gx[...].astype(BF)
    zt[0] = gx[...].T.astype(BF)
    rs0 = Scatter(0)
    rs0.begin()
    sum1 = Total(1)
    sum1.first()
    for k in range(1, half):
        rs0.step(k)
        if k == 1:
            sum1.second()
        if k == 2:
            sum1.third()
    u = rs0.end()
    pre_grad(0, zb, u)
    back_cp = copy(back.at[0], nxt.at[0], tm=sooner)
    weight_grads(0, x0, zb, u)
    sum0 = Total(0)
    sum0.first()
    for k in range(2):
        gx[:, day(k)] = gx[:, day(k)] + direct(0, k)
    sum0.second()
    back_cp.wait_recv()
    sh = shifted(0)
    for k in range(2):
        gx_ref[:, day(k)] = gx[:, day(k)] + sh[k]
    sum0.third()
    sum1.last()
    sum0.last()
    for cp in started:
        cp.wait_send()


def per_device(n, m, features, cotangent, tiles, mask, w_prev, w_cur, w_self, w_nbr, dilations):
    rows, days, c = features.shape
    wide = days * c
    half = n // 2
    share = 6 * c // n
    factor = 1.0 / float(rows * n * days * m) ** 0.5
    copies = 4 + 6 * half + 2 * (2 * (n - 1) + m - 1)
    vm = pl.BlockSpec(memory_space=pltpu.VMEM)
    sm = pl.BlockSpec(memory_space=pltpu.SMEM)
    outs = pl.pallas_call(
        functools.partial(body, n, m, n == 8, factor),
        out_shape=[
            jax.ShapeDtypeStruct((rows, wide), F32),
            jax.ShapeDtypeStruct(w_prev.shape, F32),
            jax.ShapeDtypeStruct(w_cur.shape, F32),
            jax.ShapeDtypeStruct(w_self.shape, F32),
            jax.ShapeDtypeStruct(w_nbr.shape, F32),
        ],
        in_specs=[vm, vm, vm, sm, vm, vm, vm, vm, sm],
        out_specs=[vm] * 5,
        scratch_shapes=[
            pltpu.VMEM((rows, rows * n), BF),
            pltpu.VMEM((rows, wide), BF),
            pltpu.VMEM((L, rows, wide), BF),
            pltpu.VMEM((L, rows, wide), F32),
            pltpu.VMEM((L, rows, wide), F32),
            pltpu.VMEM((L, wide, rows), BF),
            pltpu.VMEM((rows, wide), F32),
            pltpu.VMEM((rows, wide), F32),
            pltpu.VMEM((L, rows, wide), BF),
            pltpu.VMEM((2, rows, 2 * c), BF),
            pltpu.VMEM((L, rows, wide), BF),
            pltpu.VMEM((L, rows, wide), BF),
            pltpu.VMEM((L, rows, wide), BF),
            pltpu.VMEM((half, rows, wide), BF),
            pltpu.VMEM((half, rows, wide), BF),
            pltpu.VMEM((L, 2, half, wide, rows), BF),
            pltpu.VMEM((L, 2, half, wide, rows), BF),
            pltpu.VMEM((L, n, share, c), BF),
            pltpu.VMEM((L, n - 1, share, c), BF),
            pltpu.VMEM((L, m, share, c), BF),
            pltpu.VMEM((L, n, share, c), BF),
            pltpu.SemaphoreType.DMA((copies,)),
            pltpu.SemaphoreType.DMA((copies,)),
        ],
        compiler_params=pltpu.CompilerParams(
            collective_id=0, has_side_effects=True, vmem_limit_bytes=60 * 1024 * 1024),
        name="wavenet_backward",
    )(features.reshape(rows, wide), cotangent.reshape(rows, wide), tiles, mask, w_prev, w_cur,
      w_self, w_nbr, dilations)
    return (outs[0].reshape(rows, days, c), *outs[1:])


def solution(mesh):
    in_specs = (
        P("firm", "tm", None),
        P("firm", "tm", None),
        P("firm", None, None, None),
        P("firm", None),
        P(),
        P(),
        P(),
        P(),
        P(),
    )
    out_specs = (P("firm", "tm", None), P(), P(), P(), P())
    return jax.shard_map(
        functools.partial(per_device, mesh.shape["firm"], mesh.shape["tm"]),
        mesh=mesh, in_specs=in_specs, out_specs=out_specs, check_vma=False
    )
```

```python
import functools

import jax
import jax.numpy as jnp
from jax import lax
from jax.experimental import pallas as pl
from jax.experimental.pallas import tpu as pltpu
from jax.sharding import PartitionSpec as P

L = 2
BF = jnp.bfloat16
F32 = jnp.float32


def dot(a, b, ca=1, cb=0):
    return lax.dot_general(a, b, (((ca,), (cb,)), ((), ())), preferred_element_type=F32)


def body(n, m, short_fast, x_ref, cot_ref, tiles_ref, mask_ref, wp_ref, wc_ref, ws_ref,
         wn_ref, dil_ref, gx_ref, sum_ref, adj, x1, gat, th, sg, zt, acc, acc_t, uu, gx, cur,
         prv, gpre, halo, back, nxt, ag_r, ag_l, rs_out, rs_in, gp, r1, s2, fin, send, recv):
    rows, wide = x_ref.shape
    c = wide // 2
    half = n // 2
    f = lax.axis_index("firm")
    t = lax.axis_index("tm")
    if short_fast:
        fy, fz = f % 2, f // 2
    else:
        fy, fz = f // half, f % half
    pos = fz + fy * (n - 1 - 2 * fz)

    def firm_at(p):
        p = (p + 2 * n) % n
        y = p // half
        z = p + y * (n - 1 - 2 * p)
        return 2 * z + y if short_fast else y * half + z

    right = firm_at(pos + 1)
    left = firm_at(pos - 1)
    later = (t + 1) % m
    sooner = (t + m - 1) % m
    started = []

    def copy(src, dst, firm=None, tm=None):
        i = len(started)
        cp = pltpu.make_async_remote_copy(
            src_ref=src, dst_ref=dst, send_sem=send.at[i], recv_sem=recv.at[i],
            device_id=(f if firm is None else firm, t if tm is None else tm),
            device_id_type=pl.DeviceIdType.MESH)
        cp.start()
        started.append(cp)
        return cp

    barrier = pltpu.get_barrier_semaphore()
    for o in range(1, n):
        pl.semaphore_signal(barrier, inc=1, device_id=((f + o) % n, t),
                            device_id_type=pl.DeviceIdType.MESH)
    for o in range(1, m):
        pl.semaphore_signal(barrier, inc=1, device_id=(f, (t + o) % m),
                            device_id_type=pl.DeviceIdType.MESH)

    def day(k):
        return slice(k * c, (k + 1) * c)

    def block(q):
        return pl.ds(pl.multiple_of(firm_at(q) * rows, rows), rows)

    def build(q):
        first = firm_at(q) * (rows // c)

        def one(j, _):
            cols = pl.ds(pl.multiple_of((first + j) * c, c), c)
            for i in range(rows // c):
                keep = mask_ref[i, first + j].astype(F32).astype(BF)
                adj[i * c:(i + 1) * c, cols] = tiles_ref[i, first + j] * keep
            return 0

        lax.fori_loop(0, rows // c, one, 0)

    class Scatter:
        def __init__(self, w):
            self.w, self.cps = w, {}

        def send(self, dr, k, which):
            sign = 1 - 2 * dr
            p = dot(zt[self.w, day(which)], adj[:, block(pos + (half - k) * sign)])
            if (dr, k - 1, which) in self.cps:
                self.cps[dr, k - 1, which].wait_recv()
                p = p + rs_in[self.w, dr, k - 1, day(which)].astype(F32)
            rs_out[self.w, dr, k, day(which)] = p.astype(BF)
            part = pl.ds(which * c, c)
            self.cps[dr, k, which] = copy(
                rs_out.at[self.w, dr, k, part], rs_in.at[self.w, dr, k, part],
                firm=(right, left)[dr])

        def round(self, r):
            for dr in range(2):
                self.send(dr, r, dr)
            if r + 1 < half:
                for dr in range(2):
                    self.send(dr, r + 1, 1 - dr)

        def own(self):
            acc_t[...] = dot(zt[self.w], adj[:, block(pos)])

        def end(self, k):
            p = acc_t[day(k)]
            for dr in range(2):
                self.cps[dr, half - 1, k].wait_recv()
                p = p + rs_in[self.w, dr, half - 1, day(k)].astype(F32)
            uu[:, day(k)] = p.T.astype(BF)

    def current(l, x):
        for k in range(2):
            cur[k] = dot(x[:, day(k)], wc_ref[l])

    def forward(l, x):
        d1 = dil_ref[l] == 1
        h = halo[l].astype(F32)
        h = h * jnp.where(t > 0, 1.0, 0.0)
        one = jnp.where(d1, 1.0, 0.0)
        h0, h1 = h[:, day(0)], h[:, day(1)]
        prv[l, :, day(0)] = (h1 * one + h0 * (1.0 - one)).astype(BF)
        prv[l, :, day(1)] = (x[:, day(0)].astype(F32) * one + h1 * (1.0 - one)).astype(BF)
        for k in range(2):
            pre = dot(prv[l, :, day(k)], wp_ref[l]) + cur[k]
            a = jnp.tanh(pre[:, :c])
            b = 0.5 * jnp.tanh(0.5 * pre[:, c:]) + 0.5
            th[l, :, day(k)] = a
            sg[l, :, day(k)] = b
            gat[l, :, day(k)] = (a * b).astype(BF)

    def pre_grad(l, zb, scatter):
        for k in range(2):
            gg = dot(zb[:, day(k)], ws_ref[l], 1, 1)
            scatter.end(k)
            gg = gg + dot(uu[:, day(k)], wn_ref[l], 1, 1)
            a, b = th[l, :, day(k)], sg[l, :, day(k)]
            gpre[k, :, :c] = (gg * b * (1.0 - a * a)).astype(BF)
            gpre[k, :, c:] = (gg * a * b * (1.0 - b)).astype(BF)
            back[l, :, day(k)] = dot(gpre[k], wp_ref[l], 1, 1).astype(BF)

    def direct(l, k):
        return dot(gpre[k], wc_ref[l], 1, 1)

    def shifted(l):
        one = jnp.where(dil_ref[l] == 1, 1.0, 0.0)
        nb = nxt[l].astype(F32) * jnp.where(t < m - 1, 1.0, 0.0)
        n0, n1 = nb[:, day(0)], nb[:, day(1)]
        b1 = back[l, :, day(1)].astype(F32)
        return (b1 * one + n0 * (1.0 - one), n0 * one + n1 * (1.0 - one))

    def weight_grads(l, x, zb, u):
        def total(a, b):
            return dot(a[:, day(0)], b[0], 0, 0) + dot(a[:, day(1)], b[1], 0, 0)

        pieces = []
        g2 = (gpre[0], gpre[1])
        for w in (total(prv[l], g2), total(x, g2)):
            pieces += [w[:, :c], w[:, c:]]
        z2 = (zb[:, day(0)], zb[:, day(1)])
        u2 = (u[:, day(0)], u[:, day(1)])
        pieces += [total(gat[l], z2), total(gat[l], u2)]
        gp[l] = jnp.concatenate(pieces, axis=0).astype(BF).reshape(gp.shape[1:])

    class Total:
        def __init__(self, l):
            self.l = l

        def first(self):
            self.a = [copy(gp.at[self.l, (f + o) % n], r1.at[self.l, o - 1], firm=(f + o) % n)
                      for o in range(1, n)]

        def second(self):
            l = self.l
            s = gp[l, f].astype(F32)
            for o in range(1, n):
                self.a[o - 1].wait_recv()
                s = s + r1[l, o - 1].astype(F32)
            s2[l, t] = s.astype(BF)
            self.b = [copy(s2.at[l, t], s2.at[l, t], tm=(t + o) % m) for o in range(1, m)]

        def third(self):
            l = self.l
            for cp in self.b:
                cp.wait_recv()
            s = s2[l, 0].astype(F32)
            for j in range(1, m):
                s = s + s2[l, j].astype(F32)
            fin[l, f] = s.astype(BF)
            self.d = [copy(fin.at[l, f], fin.at[l, f], firm=(f + o) % n) for o in range(1, n)]

        def last(self):
            l = self.l
            for cp in self.d:
                cp.wait_recv()
            sum_ref[l] = fin[l].reshape(6 * c, c)

    zt[1] = cot_ref[...].astype(F32).T.astype(BF)
    for q in (half, half - 1, 1 - half):
        build(pos + q)
    pl.semaphore_wait(barrier, n + m - 2)
    halo_cp = copy(x_ref, halo.at[0], tm=later)
    rs1 = Scatter(1)
    rs1.round(0)
    x0 = x_ref[...]
    current(0, x0)
    for q in range(2 - half, half - 1):
        build(pos + q)
    halo_cp.wait_recv()
    forward(0, x0)

    cps = [(copy(gat.at[0], ag_r.at[0], firm=right), copy(gat.at[0], ag_l.at[0], firm=left))]
    acc[...] = dot(adj[:, block(pos)], gat[0])
    rs1.round(1)
    for s in range(1, half + 1):
        new = []
        for dr, (buf, to) in enumerate(((ag_r, right), (ag_l, left))):
            cps[s - 1][dr].wait_recv()
            if s < half - 1:
                new.append(copy(buf.at[s - 1], buf.at[s], firm=to))
            elif s == half - 1:
                part = pl.ds(dr * (rows // 2), rows // 2)
                new.append(copy(buf.at[s - 1, part], buf.at[s, part], firm=to))
        cps.append(new)
        if s < half:
            acc[...] += (dot(adj[:, block(pos - s)], ag_r[s - 1])
                         + dot(adj[:, block(pos + s)], ag_l[s - 1]))
            if s < half - 2:
                rs1.round(s + 1)
            elif s == half - 1:
                rs1.round(s)
        else:
            h = rows // 2
            far = firm_at(pos + half) * rows
            acc[...] += (dot(adj[:, pl.ds(pl.multiple_of(far, h), h)], ag_r[s - 1, :h])
                         + dot(adj[:, pl.ds(pl.multiple_of(far + h, h), h)], ag_l[s - 1, h:]))
    for k in range(2):
        mixed = (dot(gat[0, :, day(k)], ws_ref[0])
                 + dot(acc[:, day(k)].astype(BF), wn_ref[0]))
        x1[:, day(k)] = (x_ref[:, day(k)].astype(F32) + mixed).astype(BF)
    halo_cp = copy(x1, halo.at[1], tm=later)
    current(1, x1[...])
    rs1.own()
    halo_cp.wait_recv()
    forward(1, x1[...])

    cot = cot_ref[...]
    pre_grad(1, cot, rs1)
    back_cp = copy(back.at[1], nxt.at[1], tm=sooner)
    for k in range(2):
        gx[:, day(k)] = cot[:, day(k)].astype(F32) + direct(1, k)
    weight_grads(1, x1[...], cot, uu[...])
    back_cp.wait_recv()
    sh = shifted(1)
    for k in range(2):
        gx[:, day(k)] = gx[:, day(k)] + sh[k]
    zb = gx[...].astype(BF)
    zt[0] = gx[...].T.astype(BF)
    rs0 = Scatter(0)
    rs0.round(0)
    sum1 = Total(1)
    sum1.first()
    rs0.own()
    for k in range(1, half):
        rs0.round(k)
        if k == 1:
            sum1.second()
        if k == 2:
            sum1.third()
    pre_grad(0, zb, rs0)
    back_cp = copy(back.at[0], nxt.at[0], tm=sooner)
    weight_grads(0, x0, zb, uu[...])
    sum0 = Total(0)
    sum0.first()
    for k in range(2):
        gx[:, day(k)] = gx[:, day(k)] + direct(0, k)
    sum0.second()
    back_cp.wait_recv()
    sh = shifted(0)
    for k in range(2):
        gx_ref[:, day(k)] = gx[:, day(k)] + sh[k]
    sum0.third()
    sum1.last()
    sum0.last()
    for cp in started:
        cp.wait_send()


def finish(factor, gx_ref, sum_ref, out_ref, op_ref, oc_ref, os_ref, on_ref):
    c = on_ref.shape[-1]
    for k in range(2):
        out_ref[:, k, :] = gx_ref[:, k * c:(k + 1) * c]
    for l in range(L):
        g = sum_ref[l].astype(F32) * factor
        op_ref[l, :, :c] = g[:c]
        op_ref[l, :, c:] = g[c:2 * c]
        oc_ref[l, :, :c] = g[2 * c:3 * c]
        oc_ref[l, :, c:] = g[3 * c:4 * c]
        os_ref[l] = g[4 * c:5 * c]
        on_ref[l] = g[5 * c:]


def per_device(n, m, features, cotangent, tiles, mask, w_prev, w_cur, w_self, w_nbr, dilations):
    rows, days, c = features.shape
    wide = days * c
    half = n // 2
    share = 6 * c // n
    factor = 1.0 / float(rows * n * days * m) ** 0.5
    copies = 4 + 2 * half + 4 * (n - 1) + 2 * (2 * (n - 1) + m - 1)
    vm = pl.BlockSpec(memory_space=pltpu.VMEM)
    sm = pl.BlockSpec(memory_space=pltpu.SMEM)
    flow, sums = pl.pallas_call(
        functools.partial(body, n, m, n == 8),
        out_shape=[
            jax.ShapeDtypeStruct((rows, wide), F32),
            jax.ShapeDtypeStruct((L, 6 * c, c), BF),
        ],
        in_specs=[vm, vm, vm, sm, vm, vm, vm, vm, sm],
        out_specs=[vm] * 2,
        scratch_shapes=[
            pltpu.VMEM((rows, rows * n), BF),
            pltpu.VMEM((rows, wide), BF),
            pltpu.VMEM((L, rows, wide), BF),
            pltpu.VMEM((L, rows, wide), F32),
            pltpu.VMEM((L, rows, wide), F32),
            pltpu.VMEM((L, wide, rows), BF),
            pltpu.VMEM((rows, wide), F32),
            pltpu.VMEM((wide, rows), F32),
            pltpu.VMEM((rows, wide), BF),
            pltpu.VMEM((rows, wide), F32),
            pltpu.VMEM((2, rows, 2 * c), F32),
            pltpu.VMEM((L, rows, wide), BF),
            pltpu.VMEM((2, rows, 2 * c), BF),
            pltpu.VMEM((L, rows, wide), BF),
            pltpu.VMEM((L, rows, wide), BF),
            pltpu.VMEM((L, rows, wide), BF),
            pltpu.VMEM((half, rows, wide), BF),
            pltpu.VMEM((half, rows, wide), BF),
            pltpu.VMEM((L, 2, half, wide, rows), BF),
            pltpu.VMEM((L, 2, half, wide, rows), BF),
            pltpu.VMEM((L, n, share, c), BF),
            pltpu.VMEM((L, n - 1, share, c), BF),
            pltpu.VMEM((L, m, share, c), BF),
            pltpu.VMEM((L, n, share, c), BF),
            pltpu.SemaphoreType.DMA((copies,)),
            pltpu.SemaphoreType.DMA((copies,)),
        ],
        compiler_params=pltpu.CompilerParams(
            collective_id=0, has_side_effects=True, vmem_limit_bytes=60 * 1024 * 1024),
        name="wavenet_backward",
    )(features.reshape(rows, wide), cotangent.reshape(rows, wide), tiles, mask, w_prev, w_cur,
      w_self, w_nbr, dilations)
    return pl.pallas_call(
        functools.partial(finish, factor),
        out_shape=[
            jax.ShapeDtypeStruct(features.shape, F32),
            jax.ShapeDtypeStruct(w_prev.shape, F32),
            jax.ShapeDtypeStruct(w_cur.shape, F32),
            jax.ShapeDtypeStruct(w_self.shape, F32),
            jax.ShapeDtypeStruct(w_nbr.shape, F32),
        ],
        in_specs=[vm] * 2,
        out_specs=[vm] * 5,
        name="finish",
    )(flow, sums)


def solution(mesh):
    in_specs = (
        P("firm", "tm", None),
        P("firm", "tm", None),
        P("firm", None, None, None),
        P("firm", None),
        P(),
        P(),
        P(),
        P(),
        P(),
    )
    out_specs = (P("firm", "tm", None), P(), P(), P(), P())
    return jax.shard_map(
        functools.partial(per_device, mesh.shape["firm"], mesh.shape["tm"]),
        mesh=mesh, in_specs=in_specs, out_specs=out_specs, check_vma=False
    )
```

```python
import functools

import jax
import jax.numpy as jnp
from jax import lax
from jax.experimental import pallas as pl
from jax.experimental.pallas import tpu as pltpu
from jax.sharding import PartitionSpec as P

L = 2
BF = jnp.bfloat16
F32 = jnp.float32


def dot(a, b, ca=1, cb=0):
    return lax.dot_general(a, b, (((ca,), (cb,)), ((), ())), preferred_element_type=F32)


def body(n, m, short_fast, x_ref, cot_ref, tiles_ref, mask_ref, wp_ref, wc_ref, ws_ref,
         wn_ref, dil_ref, gx_ref, sum_ref, adj, x1, gat, th, sg, zt, acc, acc_t, uu, gx, zb, cur,
         prv, gpre, halo, back, nxt, ag_r, ag_l, rs_out, rs_in, gp, r1, s2, fin, send, recv):
    rows, c = x_ref.shape[1:]
    half = n // 2
    f = lax.axis_index("firm")
    t = lax.axis_index("tm")
    if short_fast:
        fy, fz = f % 2, f // 2
    else:
        fy, fz = f // half, f % half
    pos = fz + fy * (n - 1 - 2 * fz)

    def firm_at(p):
        p = (p + 2 * n) % n
        y = p // half
        z = p + y * (n - 1 - 2 * p)
        return 2 * z + y if short_fast else y * half + z

    right = firm_at(pos + 1)
    left = firm_at(pos - 1)
    later = (t + 1) % m
    sooner = (t + m - 1) % m
    started = []

    def copy(src, dst, firm=None, tm=None):
        i = len(started)
        cp = pltpu.make_async_remote_copy(
            src_ref=src, dst_ref=dst, send_sem=send.at[i], recv_sem=recv.at[i],
            device_id=(f if firm is None else firm, t if tm is None else tm),
            device_id_type=pl.DeviceIdType.MESH)
        cp.start()
        started.append(cp)
        return cp

    barrier = pltpu.get_barrier_semaphore()
    for o in range(1, n):
        pl.semaphore_signal(barrier, inc=1, device_id=((f + o) % n, t),
                            device_id_type=pl.DeviceIdType.MESH)
    for o in range(1, m):
        pl.semaphore_signal(barrier, inc=1, device_id=(f, (t + o) % m),
                            device_id_type=pl.DeviceIdType.MESH)

    def day(k):
        return slice(k * c, (k + 1) * c)

    def block(q):
        return pl.ds(pl.multiple_of(firm_at(q) * rows, rows), rows)

    def build(q):
        first = firm_at(q) * (rows // c)

        def one(j, _):
            cols = pl.ds(pl.multiple_of((first + j) * c, c), c)
            for i in range(rows // c):
                keep = mask_ref[i, first + j].astype(F32).astype(BF)
                adj[i * c:(i + 1) * c, cols] = tiles_ref[i, first + j] * keep
            return 0

        lax.fori_loop(0, rows // c, one, 0)

    class Scatter:
        def __init__(self, w):
            self.w, self.cps = w, {}

        def send(self, dr, k, which):
            sign = 1 - 2 * dr
            p = dot(zt[self.w, day(which)], adj[:, block(pos + (half - k) * sign)])
            if (dr, k - 1, which) in self.cps:
                self.cps[dr, k - 1, which].wait_recv()
                p = p + rs_in[self.w, dr, k - 1, day(which)].astype(F32)
            rs_out[self.w, dr, k, day(which)] = p.astype(BF)
            part = pl.ds(which * c, c)
            self.cps[dr, k, which] = copy(
                rs_out.at[self.w, dr, k, part], rs_in.at[self.w, dr, k, part],
                firm=(right, left)[dr])

        def round(self, r):
            for dr in range(2):
                self.send(dr, r, dr)
            if r + 1 < half:
                for dr in range(2):
                    self.send(dr, r + 1, 1 - dr)

        def own(self):
            acc_t[...] = dot(zt[self.w], adj[:, block(pos)])

        def end(self, k):
            p = acc_t[day(k)]
            for dr in range(2):
                self.cps[dr, half - 1, k].wait_recv()
                p = p + rs_in[self.w, dr, half - 1, day(k)].astype(F32)
            uu[:, day(k)] = p.T.astype(BF)

    def current(l, x):
        for k in range(2):
            cur[k] = dot(x[k], wc_ref[l])

    def forward(l, x):
        d1 = dil_ref[l] == 1
        some = jnp.where(t > 0, 1.0, 0.0)
        one = jnp.where(d1, 1.0, 0.0)
        h0, h1 = halo[l, 0].astype(F32) * some, halo[l, 1].astype(F32) * some
        prv[l, :, day(0)] = (h1 * one + h0 * (1.0 - one)).astype(BF)
        prv[l, :, day(1)] = (x[0].astype(F32) * one + h1 * (1.0 - one)).astype(BF)
        for k in range(2):
            pre = dot(prv[l, :, day(k)], wp_ref[l]) + cur[k]
            a = jnp.tanh(pre[:, :c])
            b = 0.5 * jnp.tanh(0.5 * pre[:, c:]) + 0.5
            th[l, :, day(k)] = a
            sg[l, :, day(k)] = b
            gat[l, :, day(k)] = (a * b).astype(BF)

    def pre_grad(l, zb, scatter):
        cps = []
        for k in range(2):
            gg = dot(zb[k], ws_ref[l], 1, 1)
            scatter.end(k)
            gg = gg + dot(uu[:, day(k)], wn_ref[l], 1, 1)
            a, b = th[l, :, day(k)], sg[l, :, day(k)]
            gpre[k, :, :c] = (gg * b * (1.0 - a * a)).astype(BF)
            gpre[k, :, c:] = (gg * a * b * (1.0 - b)).astype(BF)
            back[l, k] = dot(gpre[k], wp_ref[l], 1, 1).astype(BF)
            cps.append(copy(back.at[l, k], nxt.at[l, k], tm=sooner))
        return cps

    def direct(l, k):
        return dot(gpre[k], wc_ref[l], 1, 1)

    def shifted(l):
        one = jnp.where(dil_ref[l] == 1, 1.0, 0.0)
        some = jnp.where(t < m - 1, 1.0, 0.0)
        n0, n1 = nxt[l, 0].astype(F32) * some, nxt[l, 1].astype(F32) * some
        b1 = back[l, 1].astype(F32)
        return (b1 * one + n0 * (1.0 - one), n0 * one + n1 * (1.0 - one))

    def days(a):
        return a[:, day(0)], a[:, day(1)]

    def weight_grads(l, x, zb, u):
        def total(a, b):
            return dot(a[0], b[0], 0, 0) + dot(a[1], b[1], 0, 0)

        pieces = []
        g2 = (gpre[0], gpre[1])
        for w in (total(days(prv[l]), g2), total(x, g2)):
            pieces += [w[:, :c], w[:, c:]]
        g = days(gat[l])
        pieces += [total(g, zb), total(g, days(u))]
        gp[l] = jnp.concatenate(pieces, axis=0).astype(BF).reshape(gp.shape[1:])

    class Total:
        def __init__(self, l):
            self.l = l

        def first(self):
            self.a = [copy(gp.at[self.l, (f + o) % n], r1.at[self.l, o - 1], firm=(f + o) % n)
                      for o in range(1, n)]

        def second(self):
            l = self.l
            s = gp[l, f].astype(F32)
            for o in range(1, n):
                self.a[o - 1].wait_recv()
                s = s + r1[l, o - 1].astype(F32)
            s2[l, t] = s.astype(BF)
            self.b = [copy(s2.at[l, t], s2.at[l, t], tm=(t + o) % m) for o in range(1, m)]

        def third(self):
            l = self.l
            for cp in self.b:
                cp.wait_recv()
            s = s2[l, 0].astype(F32)
            for j in range(1, m):
                s = s + s2[l, j].astype(F32)
            fin[l, f] = s.astype(BF)
            self.d = [copy(fin.at[l, f], fin.at[l, f], firm=(f + o) % n) for o in range(1, n)]

        def last(self):
            l = self.l
            for cp in self.d:
                cp.wait_recv()
            sum_ref[l] = fin[l].reshape(6 * c, c)

    for k in range(2):
        zt[1, day(k)] = cot_ref[k].astype(F32).T.astype(BF)
    for q in (half, half - 1, 1 - half):
        build(pos + q)
    pl.semaphore_wait(barrier, n + m - 2)
    halo_cp = copy(x_ref, halo.at[0], tm=later)
    rs1 = Scatter(1)
    rs1.round(0)
    current(0, x_ref)
    for q in range(2 - half, half - 1):
        build(pos + q)
    halo_cp.wait_recv()
    forward(0, x_ref)

    h = rows // 2
    ring = ((ag_r, right), (ag_l, left))
    cps = {}

    def pass_on(dr, s, part):
        rng = pl.ds(part * h, h)
        buf, to = ring[dr]
        src = buf.at[s - 1, rng] if s else gat.at[0, rng]
        cps[dr, s, part] = copy(src, buf.at[s, rng], firm=to)

    for dr in range(2):
        pass_on(dr, 0, dr)
    for dr in range(2):
        pass_on(dr, 0, 1 - dr)
    acc[...] = dot(adj[:, block(pos)], gat[0])
    rs1.round(1)
    for s in range(1, half):
        for dr in range(2):
            cps[dr, s - 1, dr].wait_recv()
            pass_on(dr, s, dr)
        for dr in range(2):
            cps[dr, s - 1, 1 - dr].wait_recv()
            if s < half - 1:
                pass_on(dr, s, 1 - dr)
        acc[...] += (dot(adj[:, block(pos - s)], ag_r[s - 1])
                     + dot(adj[:, block(pos + s)], ag_l[s - 1]))
        if 1 < s < half - 2:
            rs1.round(s)
        elif s == half - 1:
            rs1.round(half - 2)
    far = firm_at(pos + half) * rows
    cps[0, half - 1, 0].wait_recv()
    cps[1, half - 1, 1].wait_recv()
    acc[...] += (dot(adj[:, pl.ds(pl.multiple_of(far, h), h)], ag_r[half - 1, :h])
                 + dot(adj[:, pl.ds(pl.multiple_of(far + h, h), h)], ag_l[half - 1, h:]))
    halo_cps = []
    for k in (1, 0):
        mixed = (dot(gat[0, :, day(k)], ws_ref[0])
                 + dot(acc[:, day(k)].astype(BF), wn_ref[0]))
        x1[k] = (x_ref[k].astype(F32) + mixed).astype(BF)
        halo_cps.append(copy(x1.at[k], halo.at[1, k], tm=later))
    current(1, x1)
    rs1.round(half - 1)
    rs1.own()
    for cp in halo_cps:
        cp.wait_recv()
    forward(1, x1)

    back_cps = pre_grad(1, cot_ref, rs1)
    for k in range(2):
        gx[k] = cot_ref[k].astype(F32) + direct(1, k)
    weight_grads(1, x1, (cot_ref[0], cot_ref[1]), uu[...])
    for cp in back_cps:
        cp.wait_recv()
    sh = shifted(1)
    for k in range(2):
        gx[k] = gx[k] + sh[k]
        zb[k] = gx[k].astype(BF)
        zt[0, day(k)] = gx[k].T.astype(BF)
    rs0 = Scatter(0)
    rs0.round(0)
    sum1 = Total(1)
    sum1.first()
    rs0.own()
    for k in range(1, half):
        rs0.round(k)
        if k == 1:
            sum1.second()
        if k == 2:
            sum1.third()
    back_cps = pre_grad(0, zb, rs0)
    weight_grads(0, x_ref, (zb[0], zb[1]), uu[...])
    sum0 = Total(0)
    sum0.first()
    for k in range(2):
        gx[k] = gx[k] + direct(0, k)
    for cp in back_cps:
        cp.wait_recv()
    sh = shifted(0)
    for k in range(2):
        gx_ref[k] = gx[k] + sh[k]
    sum0.second()
    sum0.third()
    sum1.last()
    sum0.last()
    for cp in started:
        cp.wait_send()


def finish(factor, gx_ref, sum_ref, out_ref, op_ref, oc_ref, os_ref, on_ref):
    c = on_ref.shape[-1]
    for k in range(2):
        out_ref[:, k, :] = gx_ref[k]
    for l in range(L):
        g = sum_ref[l].astype(F32) * factor
        op_ref[l, :, :c] = g[:c]
        op_ref[l, :, c:] = g[c:2 * c]
        oc_ref[l, :, :c] = g[2 * c:3 * c]
        oc_ref[l, :, c:] = g[3 * c:4 * c]
        os_ref[l] = g[4 * c:5 * c]
        on_ref[l] = g[5 * c:]


def per_device(n, m, features, cotangent, tiles, mask, w_prev, w_cur, w_self, w_nbr, dilations):
    rows, days, c = features.shape
    wide = days * c
    half = n // 2
    share = 6 * c // n
    factor = 1.0 / float(rows * n * days * m) ** 0.5
    copies = 7 + 6 * (n - 1) + 2 * (2 * (n - 1) + m - 1)
    vm = pl.BlockSpec(memory_space=pltpu.VMEM)
    sm = pl.BlockSpec(memory_space=pltpu.SMEM)
    flow, sums = pl.pallas_call(
        functools.partial(body, n, m, n == 8),
        out_shape=[
            jax.ShapeDtypeStruct((days, rows, c), F32),
            jax.ShapeDtypeStruct((L, 6 * c, c), BF),
        ],
        in_specs=[vm, vm, vm, sm, vm, vm, vm, vm, sm],
        out_specs=[vm] * 2,
        scratch_shapes=[
            pltpu.VMEM((rows, rows * n), BF),
            pltpu.VMEM((days, rows, c), BF),
            pltpu.VMEM((L, rows, wide), BF),
            pltpu.VMEM((L, rows, wide), F32),
            pltpu.VMEM((L, rows, wide), F32),
            pltpu.VMEM((L, wide, rows), BF),
            pltpu.VMEM((rows, wide), F32),
            pltpu.VMEM((wide, rows), F32),
            pltpu.VMEM((rows, wide), BF),
            pltpu.VMEM((days, rows, c), F32),
            pltpu.VMEM((days, rows, c), BF),
            pltpu.VMEM((2, rows, 2 * c), F32),
            pltpu.VMEM((L, rows, wide), BF),
            pltpu.VMEM((2, rows, 2 * c), BF),
            pltpu.VMEM((L, days, rows, c), BF),
            pltpu.VMEM((L, days, rows, c), BF),
            pltpu.VMEM((L, days, rows, c), BF),
            pltpu.VMEM((half, rows, wide), BF),
            pltpu.VMEM((half, rows, wide), BF),
            pltpu.VMEM((L, 2, half, wide, rows), BF),
            pltpu.VMEM((L, 2, half, wide, rows), BF),
            pltpu.VMEM((L, n, share, c), BF),
            pltpu.VMEM((L, n - 1, share, c), BF),
            pltpu.VMEM((L, m, share, c), BF),
            pltpu.VMEM((L, n, share, c), BF),
            pltpu.SemaphoreType.DMA((copies,)),
            pltpu.SemaphoreType.DMA((copies,)),
        ],
        compiler_params=pltpu.CompilerParams(
            collective_id=0, has_side_effects=True, vmem_limit_bytes=60 * 1024 * 1024),
        name="wavenet_backward",
    )(features.transpose(1, 0, 2), cotangent.transpose(1, 0, 2), tiles, mask, w_prev, w_cur,
      w_self, w_nbr, dilations)
    return pl.pallas_call(
        functools.partial(finish, factor),
        out_shape=[
            jax.ShapeDtypeStruct(features.shape, F32),
            jax.ShapeDtypeStruct(w_prev.shape, F32),
            jax.ShapeDtypeStruct(w_cur.shape, F32),
            jax.ShapeDtypeStruct(w_self.shape, F32),
            jax.ShapeDtypeStruct(w_nbr.shape, F32),
        ],
        in_specs=[vm] * 2,
        out_specs=[vm] * 5,
        name="finish",
    )(flow, sums)


def solution(mesh):
    in_specs = (
        P("firm", "tm", None),
        P("firm", "tm", None),
        P("firm", None, None, None),
        P("firm", None),
        P(),
        P(),
        P(),
        P(),
        P(),
    )
    out_specs = (P("firm", "tm", None), P(), P(), P(), P())
    return jax.shard_map(
        functools.partial(per_device, mesh.shape["firm"], mesh.shape["tm"]),
        mesh=mesh, in_specs=in_specs, out_specs=out_specs, check_vma=False
    )
```

```python
import functools

import jax
import jax.numpy as jnp
from jax import lax
from jax.experimental import pallas as pl
from jax.experimental.pallas import tpu as pltpu
from jax.sharding import PartitionSpec as P

L = 2
BF = jnp.bfloat16
F32 = jnp.float32


def dot(a, b, ca=1, cb=0):
    return lax.dot_general(a, b, (((ca,), (cb,)), ((), ())), preferred_element_type=F32)


def body(n, m, short_fast, x_ref, cot_ref, tiles_ref, mask_ref, wp_ref, wc_ref, ws_ref,
         wn_ref, dil_ref, gx_ref, sum_ref, adj, x1, gat, th, sg, zt, acc, acc_t, uu, gx, zb, cur,
         prv, gpre, halo, back, nxt, ag_r, ag_l, rs_out, rs_in, gp, r0, p1, r1, fin, send, recv):
    rows, c = x_ref.shape[1:]
    half = n // 2
    f = lax.axis_index("firm")
    t = lax.axis_index("tm")
    if short_fast:
        fy, fz = f % 2, f // 2
    else:
        fy, fz = f // half, f % half
    pos = fz + fy * (n - 1 - 2 * fz)

    def firm_at(p):
        p = (p + 2 * n) % n
        y = p // half
        z = p + y * (n - 1 - 2 * p)
        return 2 * z + y if short_fast else y * half + z

    right = firm_at(pos + 1)
    left = firm_at(pos - 1)
    later = (t + 1) % m
    sooner = (t + m - 1) % m
    started = []

    def copy(src, dst, firm=None, tm=None):
        i = len(started)
        cp = pltpu.make_async_remote_copy(
            src_ref=src, dst_ref=dst, send_sem=send.at[i], recv_sem=recv.at[i],
            device_id=(f if firm is None else firm, t if tm is None else tm),
            device_id_type=pl.DeviceIdType.MESH)
        cp.start()
        started.append(cp)
        return cp

    barrier = pltpu.get_barrier_semaphore()
    for o in range(1, n):
        pl.semaphore_signal(barrier, inc=1, device_id=((f + o) % n, t),
                            device_id_type=pl.DeviceIdType.MESH)
    for o in range(1, m):
        pl.semaphore_signal(barrier, inc=1, device_id=(f, (t + o) % m),
                            device_id_type=pl.DeviceIdType.MESH)

    def day(k):
        return slice(k * c, (k + 1) * c)

    def block(q):
        return pl.ds(pl.multiple_of(firm_at(q) * rows, rows), rows)

    def build(q):
        first = firm_at(q) * (rows // c)

        def one(j, _):
            cols = pl.ds(pl.multiple_of((first + j) * c, c), c)
            for i in range(rows // c):
                keep = mask_ref[i, first + j].astype(F32).astype(BF)
                adj[i * c:(i + 1) * c, cols] = tiles_ref[i, first + j] * keep
            return 0

        lax.fori_loop(0, rows // c, one, 0)

    class Scatter:
        def __init__(self, w):
            self.w, self.cps = w, {}

        def send(self, dr, k, which):
            sign = 1 - 2 * dr
            p = dot(zt[self.w, day(which)], adj[:, block(pos + (half - k) * sign)])
            if (dr, k - 1, which) in self.cps:
                self.cps[dr, k - 1, which].wait_recv()
                p = p + rs_in[self.w, dr, k - 1, day(which)].astype(F32)
            rs_out[self.w, dr, k, day(which)] = p.astype(BF)
            part = pl.ds(which * c, c)
            self.cps[dr, k, which] = copy(
                rs_out.at[self.w, dr, k, part], rs_in.at[self.w, dr, k, part],
                firm=(right, left)[dr])

        def round(self, r):
            for dr in range(2):
                self.send(dr, r, dr)
            if r + 1 < half:
                for dr in range(2):
                    self.send(dr, r + 1, 1 - dr)

        def own(self):
            acc_t[...] = dot(zt[self.w], adj[:, block(pos)])

        def end(self, k):
            p = acc_t[day(k)]
            for dr in range(2):
                self.cps[dr, half - 1, k].wait_recv()
                p = p + rs_in[self.w, dr, half - 1, day(k)].astype(F32)
            uu[:, day(k)] = p.T.astype(BF)

    def current(l, x):
        for k in range(2):
            cur[k] = dot(x[k], wc_ref[l])

    def forward(l, x):
        d1 = dil_ref[l] == 1
        some = jnp.where(t > 0, 1.0, 0.0)
        one = jnp.where(d1, 1.0, 0.0)
        h0, h1 = halo[l, 0].astype(F32) * some, halo[l, 1].astype(F32) * some
        prv[l, :, day(0)] = (h1 * one + h0 * (1.0 - one)).astype(BF)
        prv[l, :, day(1)] = (x[0].astype(F32) * one + h1 * (1.0 - one)).astype(BF)
        for k in range(2):
            pre = dot(prv[l, :, day(k)], wp_ref[l]) + cur[k]
            a = jnp.tanh(pre[:, :c])
            b = 0.5 * jnp.tanh(0.5 * pre[:, c:]) + 0.5
            th[l, :, day(k)] = a
            sg[l, :, day(k)] = b
            gat[l, :, day(k)] = (a * b).astype(BF)

    def pre_grad(l, zb, scatter):
        cps = []
        for k in range(2):
            gg = dot(zb[k], ws_ref[l], 1, 1)
            scatter.end(k)
            gg = gg + dot(uu[:, day(k)], wn_ref[l], 1, 1)
            a, b = th[l, :, day(k)], sg[l, :, day(k)]
            gpre[k, :, :c] = (gg * b * (1.0 - a * a)).astype(BF)
            gpre[k, :, c:] = (gg * a * b * (1.0 - b)).astype(BF)
            back[l, k] = dot(gpre[k], wp_ref[l], 1, 1).astype(BF)
            cps.append(copy(back.at[l, k], nxt.at[l, k], tm=sooner))
        return cps

    def direct(l, k):
        return dot(gpre[k], wc_ref[l], 1, 1)

    def shifted(l):
        one = jnp.where(dil_ref[l] == 1, 1.0, 0.0)
        some = jnp.where(t < m - 1, 1.0, 0.0)
        n0, n1 = nxt[l, 0].astype(F32) * some, nxt[l, 1].astype(F32) * some
        b1 = back[l, 1].astype(F32)
        return (b1 * one + n0 * (1.0 - one), n0 * one + n1 * (1.0 - one))

    def days(a):
        return a[:, day(0)], a[:, day(1)]

    def weight_grads(l, x, zb, u):
        def total(a, b):
            return dot(a[0], b[0], 0, 0) + dot(a[1], b[1], 0, 0)

        pieces = []
        g2 = (gpre[0], gpre[1])
        for w in (total(days(prv[l]), g2), total(x, g2)):
            pieces += [w[:, :c], w[:, c:]]
        g = days(gat[l])
        pieces += [total(g, zb), total(g, days(u))]
        spare = gp.shape[1] * gp.shape[2] * gp.shape[3] - 6 * c
        if spare:
            pieces.append(jnp.zeros((spare, c), F32))
        gp[l] = jnp.concatenate(pieces, axis=0).astype(BF).reshape(gp.shape[1:])

    class Total:
        def __init__(self, l):
            self.l = l

        def first(self):
            l = self.l
            self.a = [copy(gp.at[l, (t + o) % m], r0.at[l, o - 1], tm=(t + o) % m)
                      for o in range(1, m)]

        def second(self):
            l = self.l
            s = gp[l, t].astype(F32)
            for o in range(1, m):
                self.a[o - 1].wait_recv()
                s = s + r0[l, o - 1].astype(F32)
            p1[l] = s.astype(BF)
            self.b = [copy(p1.at[l, (f + o) % n], r1.at[l, o - 1], firm=(f + o) % n)
                      for o in range(1, n)]

        def third(self):
            l = self.l
            s = p1[l, f].astype(F32)
            for o in range(1, n):
                self.b[o - 1].wait_recv()
                s = s + r1[l, o - 1].astype(F32)
            fin[l, t, f] = s.astype(BF)
            self.d = [copy(fin.at[l, t, f], fin.at[l, t, f], firm=(f + o) % n)
                      for o in range(1, n)]

        def fourth(self):
            l = self.l
            for cp in self.d:
                cp.wait_recv()
            self.e = [copy(fin.at[l, t], fin.at[l, t], tm=(t + o) % m) for o in range(1, m)]

        def last(self):
            l = self.l
            for cp in self.e:
                cp.wait_recv()
            sum_ref[l] = fin[l].reshape(-1, c)[:6 * c]

    for k in range(2):
        zt[1, day(k)] = cot_ref[k].astype(F32).T.astype(BF)
    for q in (half, half - 1, 1 - half):
        build(pos + q)
    pl.semaphore_wait(barrier, n + m - 2)
    halo_cp = copy(x_ref, halo.at[0], tm=later)
    rs1 = Scatter(1)
    rs1.round(0)
    current(0, x_ref)
    for q in range(2 - half, half - 1):
        build(pos + q)
    halo_cp.wait_recv()
    forward(0, x_ref)

    h = rows // 2
    ring = ((ag_r, right), (ag_l, left))
    cps = {}

    def pass_on(dr, s, part):
        rng = pl.ds(part * h, h)
        buf, to = ring[dr]
        src = buf.at[s - 1, rng] if s else gat.at[0, rng]
        cps[dr, s, part] = copy(src, buf.at[s, rng], firm=to)

    for dr in range(2):
        pass_on(dr, 0, dr)
    for dr in range(2):
        pass_on(dr, 0, 1 - dr)
    acc[...] = dot(adj[:, block(pos)], gat[0])
    rs1.round(1)
    for s in range(1, half):
        for dr in range(2):
            cps[dr, s - 1, dr].wait_recv()
            pass_on(dr, s, dr)
        for dr in range(2):
            cps[dr, s - 1, 1 - dr].wait_recv()
            if s < half - 1:
                pass_on(dr, s, 1 - dr)
        acc[...] += (dot(adj[:, block(pos - s)], ag_r[s - 1])
                     + dot(adj[:, block(pos + s)], ag_l[s - 1]))
        if 1 < s < half - 2:
            rs1.round(s)
        elif s == half - 1:
            rs1.round(half - 2)
    far = firm_at(pos + half) * rows
    cps[0, half - 1, 0].wait_recv()
    cps[1, half - 1, 1].wait_recv()
    acc[...] += (dot(adj[:, pl.ds(pl.multiple_of(far, h), h)], ag_r[half - 1, :h])
                 + dot(adj[:, pl.ds(pl.multiple_of(far + h, h), h)], ag_l[half - 1, h:]))
    halo_cps = []
    for k in (1, 0):
        mixed = (dot(gat[0, :, day(k)], ws_ref[0])
                 + dot(acc[:, day(k)].astype(BF), wn_ref[0]))
        x1[k] = (x_ref[k].astype(F32) + mixed).astype(BF)
        halo_cps.append(copy(x1.at[k], halo.at[1, k], tm=later))
    current(1, x1)
    rs1.round(half - 1)
    rs1.own()
    for cp in halo_cps:
        cp.wait_recv()
    forward(1, x1)

    back_cps = pre_grad(1, cot_ref, rs1)
    for k in range(2):
        gx[k] = cot_ref[k].astype(F32) + direct(1, k)
    weight_grads(1, x1, (cot_ref[0], cot_ref[1]), uu[...])
    for cp in back_cps:
        cp.wait_recv()
    sh = shifted(1)
    for k in range(2):
        gx[k] = gx[k] + sh[k]
        zb[k] = gx[k].astype(BF)
        zt[0, day(k)] = gx[k].T.astype(BF)
    rs0 = Scatter(0)
    rs0.round(0)
    sum1 = Total(1)
    sum1.first()
    rs0.own()
    for k in range(1, half):
        rs0.round(k)
        if k == 1:
            sum1.second()
        if k == 2:
            sum1.third()
        if k == half - 1:
            sum1.fourth()
    back_cps = pre_grad(0, zb, rs0)
    weight_grads(0, x_ref, (zb[0], zb[1]), uu[...])
    sum0 = Total(0)
    sum0.first()
    for k in range(2):
        gx[k] = gx[k] + direct(0, k)
    for cp in back_cps:
        cp.wait_recv()
    sh = shifted(0)
    for k in range(2):
        gx_ref[k] = gx[k] + sh[k]
    sum0.second()
    sum0.third()
    sum1.last()
    sum0.fourth()
    sum0.last()
    for cp in started:
        cp.wait_send()


def finish(factor, gx_ref, sum_ref, out_ref, op_ref, oc_ref, os_ref, on_ref):
    c = on_ref.shape[-1]
    for k in range(2):
        out_ref[:, k, :] = gx_ref[k]
    for l in range(L):
        g = sum_ref[l].astype(F32) * factor
        op_ref[l, :, :c] = g[:c]
        op_ref[l, :, c:] = g[c:2 * c]
        oc_ref[l, :, :c] = g[2 * c:3 * c]
        oc_ref[l, :, c:] = g[3 * c:4 * c]
        os_ref[l] = g[4 * c:5 * c]
        on_ref[l] = g[5 * c:]


def per_device(n, m, features, cotangent, tiles, mask, w_prev, w_cur, w_self, w_nbr, dilations):
    rows, days, c = features.shape
    wide = days * c
    half = n // 2
    share = -(-6 * c // (n * m * 16)) * 16
    factor = 1.0 / float(rows * n * days * m) ** 0.5
    copies = 7 + 6 * (n - 1) + 4 * (n - 1 + m - 1)
    vm = pl.BlockSpec(memory_space=pltpu.VMEM)
    sm = pl.BlockSpec(memory_space=pltpu.SMEM)
    flow, sums = pl.pallas_call(
        functools.partial(body, n, m, n == 8),
        out_shape=[
            jax.ShapeDtypeStruct((days, rows, c), F32),
            jax.ShapeDtypeStruct((L, 6 * c, c), BF),
        ],
        in_specs=[vm, vm, vm, sm, vm, vm, vm, vm, sm],
        out_specs=[vm] * 2,
        scratch_shapes=[
            pltpu.VMEM((rows, rows * n), BF),
            pltpu.VMEM((days, rows, c), BF),
            pltpu.VMEM((L, rows, wide), BF),
            pltpu.VMEM((L, rows, wide), F32),
            pltpu.VMEM((L, rows, wide), F32),
            pltpu.VMEM((L, wide, rows), BF),
            pltpu.VMEM((rows, wide), F32),
            pltpu.VMEM((wide, rows), F32),
            pltpu.VMEM((rows, wide), BF),
            pltpu.VMEM((days, rows, c), F32),
            pltpu.VMEM((days, rows, c), BF),
            pltpu.VMEM((2, rows, 2 * c), F32),
            pltpu.VMEM((L, rows, wide), BF),
            pltpu.VMEM((2, rows, 2 * c), BF),
            pltpu.VMEM((L, days, rows, c), BF),
            pltpu.VMEM((L, days, rows, c), BF),
            pltpu.VMEM((L, days, rows, c), BF),
            pltpu.VMEM((half, rows, wide), BF),
            pltpu.VMEM((half, rows, wide), BF),
            pltpu.VMEM((L, 2, half, wide, rows), BF),
            pltpu.VMEM((L, 2, half, wide, rows), BF),
            pltpu.VMEM((L, m, n, share, c), BF),
            pltpu.VMEM((L, m - 1, n, share, c), BF),
            pltpu.VMEM((L, n, share, c), BF),
            pltpu.VMEM((L, n - 1, share, c), BF),
            pltpu.VMEM((L, m, n, share, c), BF),
            pltpu.SemaphoreType.DMA((copies,)),
            pltpu.SemaphoreType.DMA((copies,)),
        ],
        compiler_params=pltpu.CompilerParams(
            collective_id=0, has_side_effects=True, vmem_limit_bytes=60 * 1024 * 1024),
        name="wavenet_backward",
    )(features.transpose(1, 0, 2), cotangent.transpose(1, 0, 2), tiles, mask, w_prev, w_cur,
      w_self, w_nbr, dilations)
    return pl.pallas_call(
        functools.partial(finish, factor),
        out_shape=[
            jax.ShapeDtypeStruct(features.shape, F32),
            jax.ShapeDtypeStruct(w_prev.shape, F32),
            jax.ShapeDtypeStruct(w_cur.shape, F32),
            jax.ShapeDtypeStruct(w_self.shape, F32),
            jax.ShapeDtypeStruct(w_nbr.shape, F32),
        ],
        in_specs=[vm] * 2,
        out_specs=[vm] * 5,
        name="finish",
    )(flow, sums)


def solution(mesh):
    in_specs = (
        P("firm", "tm", None),
        P("firm", "tm", None),
        P("firm", None, None, None),
        P("firm", None),
        P(),
        P(),
        P(),
        P(),
        P(),
    )
    out_specs = (P("firm", "tm", None), P(), P(), P(), P())
    return jax.shard_map(
        functools.partial(per_device, mesh.shape["firm"], mesh.shape["tm"]),
        mesh=mesh, in_specs=in_specs, out_specs=out_specs, check_vma=False
    )
```

```python
import functools

import jax
import jax.numpy as jnp
from jax import lax
from jax.experimental import pallas as pl
from jax.experimental.pallas import tpu as pltpu
from jax.sharding import PartitionSpec as P

L = 2
BF = jnp.bfloat16
F32 = jnp.float32


def dot(a, b, ca=1, cb=0):
    return lax.dot_general(a, b, (((ca,), (cb,)), ((), ())), preferred_element_type=F32)


def body(n, m, short_fast, x_ref, cot_ref, tiles_ref, mask_ref, wp_ref, wc_ref, ws_ref,
         wn_ref, dil_ref, gx_ref, sum_ref, adj, x1, gat, th, sg, zt, acc, acc_t, uu, gx, zb, cur,
         prv, gpre, halo, back, nxt, ag_r, ag_l, rs_out, rs_in, gp, r0, p1, r1, fin, send, recv):
    rows, c = x_ref.shape[1:]
    half = n // 2
    f = lax.axis_index("firm")
    t = lax.axis_index("tm")
    if short_fast:
        fy, fz = f % 2, f // 2
    else:
        fy, fz = f // half, f % half
    pos = fz + fy * (n - 1 - 2 * fz)

    def firm_at(p):
        p = (p + 2 * n) % n
        y = p // half
        z = p + y * (n - 1 - 2 * p)
        return 2 * z + y if short_fast else y * half + z

    right = firm_at(pos + 1)
    left = firm_at(pos - 1)
    later = (t + 1) % m
    sooner = (t + m - 1) % m
    started = []

    def copy(src, dst, firm=None, tm=None):
        i = len(started)
        cp = pltpu.make_async_remote_copy(
            src_ref=src, dst_ref=dst, send_sem=send.at[i], recv_sem=recv.at[i],
            device_id=(f if firm is None else firm, t if tm is None else tm),
            device_id_type=pl.DeviceIdType.MESH)
        cp.start()
        started.append(cp)
        return cp

    barrier = pltpu.get_barrier_semaphore()
    for o in range(1, n):
        pl.semaphore_signal(barrier, inc=1, device_id=((f + o) % n, t),
                            device_id_type=pl.DeviceIdType.MESH)
    for o in range(1, m):
        pl.semaphore_signal(barrier, inc=1, device_id=(f, (t + o) % m),
                            device_id_type=pl.DeviceIdType.MESH)

    def day(k):
        return slice(k * c, (k + 1) * c)

    def block(q):
        return pl.ds(pl.multiple_of(firm_at(q) * rows, rows), rows)

    def build(q):
        first = firm_at(q) * (rows // c)

        def one(j, _):
            cols = pl.ds(pl.multiple_of((first + j) * c, c), c)
            for i in range(rows // c):
                keep = mask_ref[i, first + j].astype(F32).astype(BF)
                adj[i * c:(i + 1) * c, cols] = tiles_ref[i, first + j] * keep
            return 0

        lax.fori_loop(0, rows // c, one, 0)

    class Scatter:
        def __init__(self, w):
            self.w, self.cps = w, {}

        def send(self, dr, k, which):
            sign = 1 - 2 * dr
            p = dot(zt[self.w, day(which)], adj[:, block(pos + (half - k) * sign)])
            if (dr, k - 1, which) in self.cps:
                self.cps[dr, k - 1, which].wait_recv()
                p = p + rs_in[self.w, dr, k - 1, day(which)].astype(F32)
            rs_out[self.w, dr, k, day(which)] = p.astype(BF)
            part = pl.ds(which * c, c)
            self.cps[dr, k, which] = copy(
                rs_out.at[self.w, dr, k, part], rs_in.at[self.w, dr, k, part],
                firm=(right, left)[dr])

        def round(self, r):
            for dr in range(2):
                self.send(dr, r, dr)
            if r + 1 < half:
                for dr in range(2):
                    self.send(dr, r + 1, 1 - dr)

        def own(self):
            acc_t[...] = dot(zt[self.w], adj[:, block(pos)])

        def end(self, k):
            p = acc_t[day(k)]
            for dr in range(2):
                self.cps[dr, half - 1, k].wait_recv()
                p = p + rs_in[self.w, dr, half - 1, day(k)].astype(F32)
            uu[:, day(k)] = p.T.astype(BF)

    def current(l, x):
        for k in range(2):
            cur[k] = dot(x[k], wc_ref[l])

    def forward(l, x):
        d1 = dil_ref[l] == 1
        some = jnp.where(t > 0, 1.0, 0.0)
        one = jnp.where(d1, 1.0, 0.0)
        h0, h1 = halo[l, 0].astype(F32) * some, halo[l, 1].astype(F32) * some
        prv[l, :, day(0)] = (h1 * one + h0 * (1.0 - one)).astype(BF)
        prv[l, :, day(1)] = (x[0].astype(F32) * one + h1 * (1.0 - one)).astype(BF)
        for k in range(2):
            pre = dot(prv[l, :, day(k)], wp_ref[l]) + cur[k]
            a = jnp.tanh(pre[:, :c])
            b = 0.5 * jnp.tanh(0.5 * pre[:, c:]) + 0.5
            th[l, :, day(k)] = a
            sg[l, :, day(k)] = b
            gat[l, :, day(k)] = (a * b).astype(BF)

    def pre_grad(l, zb, scatter):
        cps = []
        for k in range(2):
            gg = dot(zb[k], ws_ref[l], 1, 1)
            scatter.end(k)
            gg = gg + dot(uu[:, day(k)], wn_ref[l], 1, 1)
            a, b = th[l, :, day(k)], sg[l, :, day(k)]
            gpre[k, :, :c] = (gg * b * (1.0 - a * a)).astype(BF)
            gpre[k, :, c:] = (gg * a * b * (1.0 - b)).astype(BF)
            back[l, k] = dot(gpre[k], wp_ref[l], 1, 1).astype(BF)
            cps.append(copy(back.at[l, k], nxt.at[l, k], tm=sooner))
        return cps

    def direct(l, k):
        return dot(gpre[k], wc_ref[l], 1, 1)

    def shifted(l):
        one = jnp.where(dil_ref[l] == 1, 1.0, 0.0)
        some = jnp.where(t < m - 1, 1.0, 0.0)
        n0, n1 = nxt[l, 0].astype(F32) * some, nxt[l, 1].astype(F32) * some
        b1 = back[l, 1].astype(F32)
        return (b1 * one + n0 * (1.0 - one), n0 * one + n1 * (1.0 - one))

    def days(a):
        return a[:, day(0)], a[:, day(1)]

    def weight_grads(l, x, zb, u):
        def total(a, b):
            return dot(a[0], b[0], 0, 0) + dot(a[1], b[1], 0, 0)

        pieces = []
        g2 = (gpre[0], gpre[1])
        for w in (total(days(prv[l]), g2), total(x, g2)):
            pieces += [w[:, :c], w[:, c:]]
        g = days(gat[l])
        pieces += [total(g, zb), total(g, days(u))]
        spare = gp.shape[1] * gp.shape[2] * gp.shape[3] - 6 * c
        if spare:
            pieces.append(jnp.zeros((spare, c), F32))
        gp[l] = jnp.concatenate(pieces, axis=0).astype(BF).reshape(gp.shape[1:])

    class Total:
        def __init__(self, l):
            self.l = l

        def first(self):
            l = self.l
            self.a = [copy(gp.at[l, (t + o) % m], r0.at[l, o - 1], tm=(t + o) % m)
                      for o in range(1, m)]

        def second(self):
            l = self.l
            s = gp[l, t].astype(F32)
            for o in range(1, m):
                self.a[o - 1].wait_recv()
                s = s + r0[l, o - 1].astype(F32)
            p1[l] = s.astype(BF)
            self.b = [copy(p1.at[l, (f + o) % n], r1.at[l, o - 1], firm=(f + o) % n)
                      for o in range(1, n)]

        def third(self):
            l = self.l
            s = p1[l, f].astype(F32)
            for o in range(1, n):
                self.b[o - 1].wait_recv()
                s = s + r1[l, o - 1].astype(F32)
            fin[l, t, f] = s.astype(BF)
            self.d = [copy(fin.at[l, t, f], fin.at[l, t, f], firm=(f + o) % n)
                      for o in range(1, n)]

        def fourth(self):
            l = self.l
            for cp in self.d:
                cp.wait_recv()
            self.e = [copy(fin.at[l, t], fin.at[l, t], tm=(t + o) % m) for o in range(1, m)]

        def last(self):
            l = self.l
            for cp in self.e:
                cp.wait_recv()
            sum_ref[l] = fin[l].reshape(-1, c)[:6 * c]

    for k in range(2):
        zt[1, day(k)] = cot_ref[k].astype(F32).T.astype(BF)
    for q in (half, half - 1, 1 - half):
        build(pos + q)
    pl.semaphore_wait(barrier, n + m - 2)
    halo_cp = copy(x_ref, halo.at[0], tm=later)
    rs1 = Scatter(1)
    rs1.round(0)
    current(0, x_ref)
    for q in range(2 - half, half - 1):
        build(pos + q)
    halo_cp.wait_recv()
    forward(0, x_ref)

    h = rows // 2
    ring = ((ag_r, right), (ag_l, left))
    cps = {}

    def pass_on(dr, s, part):
        rng = pl.ds(part * h, h)
        buf, to = ring[dr]
        src = buf.at[s - 1, rng] if s else gat.at[0, rng]
        cps[dr, s, part] = copy(src, buf.at[s, rng], firm=to)

    for dr in range(2):
        pass_on(dr, 0, dr)
    for dr in range(2):
        pass_on(dr, 0, 1 - dr)
    acc[...] = dot(adj[:, block(pos)], gat[0])
    rs1.round(1)
    for s in range(1, half):
        for dr in range(2):
            cps[dr, s - 1, dr].wait_recv()
            pass_on(dr, s, dr)
        for dr in range(2):
            cps[dr, s - 1, 1 - dr].wait_recv()
            if s < half - 1:
                pass_on(dr, s, 1 - dr)
        acc[...] += (dot(adj[:, block(pos - s)], ag_r[s - 1])
                     + dot(adj[:, block(pos + s)], ag_l[s - 1]))
        if 1 < s < half - 2:
            rs1.round(s)
        elif s == half - 1:
            rs1.round(half - 2)
    far = firm_at(pos + half) * rows
    cps[0, half - 1, 0].wait_recv()
    cps[1, half - 1, 1].wait_recv()
    acc[...] += (dot(adj[:, pl.ds(pl.multiple_of(far, h), h)], ag_r[half - 1, :h])
                 + dot(adj[:, pl.ds(pl.multiple_of(far + h, h), h)], ag_l[half - 1, h:]))
    halo_cps = []
    for k in (1, 0):
        mixed = (dot(gat[0, :, day(k)], ws_ref[0])
                 + dot(acc[:, day(k)].astype(BF), wn_ref[0]))
        x1[k] = (x_ref[k].astype(F32) + mixed).astype(BF)
        halo_cps.append(copy(x1.at[k], halo.at[1, k], tm=later))
    current(1, x1)
    rs1.round(half - 1)
    rs1.own()
    for cp in halo_cps:
        cp.wait_recv()
    forward(1, x1)

    back_cps = pre_grad(1, cot_ref, rs1)
    for k in range(2):
        gx[k] = cot_ref[k].astype(F32) + direct(1, k)
    for cp in back_cps:
        cp.wait_recv()
    sh = shifted(1)
    for k in range(2):
        gx[k] = gx[k] + sh[k]
        zb[k] = gx[k].astype(BF)
        zt[0, day(k)] = gx[k].T.astype(BF)
    rs0 = Scatter(0)
    rs0.round(0)
    weight_grads(1, x1, (cot_ref[0], cot_ref[1]), uu[...])
    sum1 = Total(1)
    sum1.first()
    rs0.own()
    for k in range(1, half):
        rs0.round(k)
        if k == 1:
            sum1.second()
        if k == 2:
            sum1.third()
        if k == half - 1:
            sum1.fourth()
    back_cps = pre_grad(0, zb, rs0)
    weight_grads(0, x_ref, (zb[0], zb[1]), uu[...])
    sum0 = Total(0)
    sum0.first()
    for k in range(2):
        gx[k] = gx[k] + direct(0, k)
    for cp in back_cps:
        cp.wait_recv()
    sh = shifted(0)
    for k in range(2):
        gx_ref[k] = gx[k] + sh[k]
    sum0.second()
    sum0.third()
    sum1.last()
    sum0.fourth()
    sum0.last()
    for cp in started:
        cp.wait_send()


def finish(factor, gx_ref, sum_ref, out_ref, op_ref, oc_ref, os_ref, on_ref):
    c = on_ref.shape[-1]
    for k in range(2):
        out_ref[:, k, :] = gx_ref[k]
    for l in range(L):
        g = sum_ref[l].astype(F32) * factor
        op_ref[l, :, :c] = g[:c]
        op_ref[l, :, c:] = g[c:2 * c]
        oc_ref[l, :, :c] = g[2 * c:3 * c]
        oc_ref[l, :, c:] = g[3 * c:4 * c]
        os_ref[l] = g[4 * c:5 * c]
        on_ref[l] = g[5 * c:]


def per_device(n, m, features, cotangent, tiles, mask, w_prev, w_cur, w_self, w_nbr, dilations):
    rows, days, c = features.shape
    wide = days * c
    half = n // 2
    share = -(-6 * c // (n * m * 16)) * 16
    factor = 1.0 / float(rows * n * days * m) ** 0.5
    copies = 7 + 6 * (n - 1) + 4 * (n - 1 + m - 1)
    vm = pl.BlockSpec(memory_space=pltpu.VMEM)
    sm = pl.BlockSpec(memory_space=pltpu.SMEM)
    flow, sums = pl.pallas_call(
        functools.partial(body, n, m, n == 8),
        out_shape=[
            jax.ShapeDtypeStruct((days, rows, c), F32),
            jax.ShapeDtypeStruct((L, 6 * c, c), BF),
        ],
        in_specs=[vm, vm, vm, sm, vm, vm, vm, vm, sm],
        out_specs=[vm] * 2,
        scratch_shapes=[
            pltpu.VMEM((rows, rows * n), BF),
            pltpu.VMEM((days, rows, c), BF),
            pltpu.VMEM((L, rows, wide), BF),
            pltpu.VMEM((L, rows, wide), F32),
            pltpu.VMEM((L, rows, wide), F32),
            pltpu.VMEM((L, wide, rows), BF),
            pltpu.VMEM((rows, wide), F32),
            pltpu.VMEM((wide, rows), F32),
            pltpu.VMEM((rows, wide), BF),
            pltpu.VMEM((days, rows, c), F32),
            pltpu.VMEM((days, rows, c), BF),
            pltpu.VMEM((2, rows, 2 * c), F32),
            pltpu.VMEM((L, rows, wide), BF),
            pltpu.VMEM((2, rows, 2 * c), BF),
            pltpu.VMEM((L, days, rows, c), BF),
            pltpu.VMEM((L, days, rows, c), BF),
            pltpu.VMEM((L, days, rows, c), BF),
            pltpu.VMEM((half, rows, wide), BF),
            pltpu.VMEM((half, rows, wide), BF),
            pltpu.VMEM((L, 2, half, wide, rows), BF),
            pltpu.VMEM((L, 2, half, wide, rows), BF),
            pltpu.VMEM((L, m, n, share, c), BF),
            pltpu.VMEM((L, m - 1, n, share, c), BF),
            pltpu.VMEM((L, n, share, c), BF),
            pltpu.VMEM((L, n - 1, share, c), BF),
            pltpu.VMEM((L, m, n, share, c), BF),
            pltpu.SemaphoreType.DMA((copies,)),
            pltpu.SemaphoreType.DMA((copies,)),
        ],
        compiler_params=pltpu.CompilerParams(
            collective_id=0, has_side_effects=True, vmem_limit_bytes=60 * 1024 * 1024),
        name="wavenet_backward",
    )(features.transpose(1, 0, 2), cotangent.transpose(1, 0, 2), tiles, mask, w_prev, w_cur,
      w_self, w_nbr, dilations)
    return pl.pallas_call(
        functools.partial(finish, factor),
        out_shape=[
            jax.ShapeDtypeStruct(features.shape, F32),
            jax.ShapeDtypeStruct(w_prev.shape, F32),
            jax.ShapeDtypeStruct(w_cur.shape, F32),
            jax.ShapeDtypeStruct(w_self.shape, F32),
            jax.ShapeDtypeStruct(w_nbr.shape, F32),
        ],
        in_specs=[vm] * 2,
        out_specs=[vm] * 5,
        name="finish",
    )(flow, sums)


def solution(mesh):
    in_specs = (
        P("firm", "tm", None),
        P("firm", "tm", None),
        P("firm", None, None, None),
        P("firm", None),
        P(),
        P(),
        P(),
        P(),
        P(),
    )
    out_specs = (P("firm", "tm", None), P(), P(), P(), P())
    return jax.shard_map(
        functools.partial(per_device, mesh.shape["firm"], mesh.shape["tm"]),
        mesh=mesh, in_specs=in_specs, out_specs=out_specs, check_vma=False
    )
```
